256 devices in a mesh: tm: 32 (over z, x_hi, core), comp: 8 (over y, x_lo).
Axes of the slice: x: 4 (x_hi: 2, x_lo: 2; x = x_hi * 2 + x_lo), y: 4, z: 8, core: 2. Of those that a mesh axis runs over, the one named last changes fastest.
Arguments:
- velocities: bfloat16 [8192, 3, 4096], P('tm', None, 'comp'), may hold values from -6 to 6
- atom_mask: int32 [4096], P('comp'), may hold values 0 or 1
- valid_frames: int32 [1], replicated, may hold values from 7936 to 8192
Outputs:
- correlation: float32 [256, 4096], P('tm', 'comp')
- average: float32 [256], P('tm')
The draws below stay inside these ranges and needn't reach their ends.
All inputs are finite; a program needn't handle non-finite values. No bound on the sum of `atom_mask` on one device may be relied on, other than what follows from the above.
Results may differ from the reference program's by a relative error of at most 0.0003.
Values may be sent and summed in bfloat16 or wider, within the bound.
No kernel may reach another device: no remote copies, remote signals or barrier semaphores. Data moves between devices by JAX's collectives and lax.ppermute only.
A program may use at most 64 MiB of HBM per device.

```python
import math
import jax
import jax.numpy as jnp
from jax import lax

LAGS = 256
FR_DEV = 256
FRAMES = 8192
ATOMS = 4096


def draw_velocities(key, part):
    keys = jax.random.split(key, 5)
    drift = 0.6 * jax.random.normal(keys[0], (1, 3, ATOMS), jnp.float32)
    amplitude = jax.random.uniform(keys[1], (1, 3, ATOMS), jnp.float32, 0.7, 1.3)
    noise = 0.5 * jax.random.normal(keys[2], (FRAMES, 3, ATOMS), jnp.float32)
    frequency = jax.random.randint(keys[3], (ATOMS,), FRAMES // 32, 2 * FRAMES // 5 + 1, jnp.int32)
    phase = jax.random.uniform(keys[4], (1, 3, ATOMS), jnp.float32, -math.pi, math.pi)
    ticks = jnp.arange(FRAMES, dtype=jnp.int32)[:, None] * frequency[None, :] % FRAMES
    angle = ticks.astype(jnp.float32) * (2.0 * math.pi / FRAMES)
    values = drift + amplitude * jnp.cos(angle[:, None, :] + phase) + noise
    values = jnp.clip(values, -6.0, 6.0)
    return values.astype(jnp.bfloat16)


def place_ends(entries, stream_key, low, high):
    longest = entries.shape.index(max(entries.shape))
    spots = []
    for shift in (0, 1):
        where = [jax.random.randint(jax.random.fold_in(stream_key, axis), (), 0, length) for axis, length in enumerate(entries.shape)]
        where[longest] = (where[longest] + shift) % entries.shape[longest]
        spots.append(tuple(where))
    return entries.at[spots[0]].set(low).at[spots[1]].set(high)


def setup_inputs(seed: int = 0) -> dict:
    seeds = jax.random.split(jax.random.key(seed), 4)
    return {
        "velocities": draw_velocities(jax.random.fold_in(seeds[3], 71), 0),
        "atom_mask": place_ends((jax.random.randint(seeds[1], (ATOMS,), 0, 8) < 7).astype(jnp.int32), jax.random.fold_in(seeds[1], 1), 0, 1),
        "valid_frames": jax.random.randint(seeds[2], (1,), FRAMES - 2 * FR_DEV + LAGS, FRAMES + 1).astype(jnp.int32),
    }


def reference(velocities, atom_mask, valid_frames):
    frame_count = velocities.shape[0]
    last_valid = valid_frames[0]
    in_range = jnp.arange(frame_count, dtype=jnp.int32) < last_valid
    clean = jnp.where(in_range[:, None, None], velocities, jnp.zeros_like(velocities))
    padded = jnp.concatenate([clean, jnp.zeros((LAGS, clean.shape[1], clean.shape[2]), clean.dtype)], 0)

    def per_offset(offset):
        shifted = lax.dynamic_slice_in_dim(padded, offset, frame_count, 0)
        return jnp.sum(clean.astype(jnp.float32) * shifted.astype(jnp.float32), axis=(0, 1))

    lag_sums = lax.map(per_offset, jnp.arange(LAGS, dtype=jnp.int32))
    anchors = (last_valid - jnp.arange(LAGS, dtype=jnp.int32)).astype(jnp.float32)
    atom_weight = atom_mask.astype(jnp.float32)
    correlation = atom_weight[None, :] * lag_sums / anchors[:, None]
    average = jnp.sum(correlation, axis=1) / jnp.maximum(jnp.sum(atom_weight), 1.0)
    return correlation, average
```

```python
import jax
import jax.numpy as jnp
import ml_dtypes
import numpy as np
from jax import lax
from jax.experimental import pallas as pl
from jax.experimental.pallas import tpu as pltpu
from jax.sharding import PartitionSpec as P

LAGS = 256
FRAMES = 256
SIZE = 512
LANES = 128
GROUP = 4


def two_parts(table):
    high = table.astype(ml_dtypes.bfloat16)
    low = (table - high.astype(np.float64)).astype(ml_dtypes.bfloat16)
    return high, low


def tables():
    f = np.concatenate([np.arange(0, SIZE // 2, 2), np.arange(1, SIZE // 2, 2)])
    angle = 2.0 * np.pi * (f + 0.5) / SIZE
    ahead = angle[:, None] * np.arange(FRAMES)[None, :]
    forward = np.concatenate([np.cos(ahead), -np.sin(ahead)], 0)
    back = angle[None, :] * np.arange(LAGS)[:, None]
    inverse = np.concatenate([np.cos(back), -np.sin(back)], 1) * (2.0 / SIZE)
    return two_parts(forward), two_parts(inverse)


def dot(a, b):
    return jnp.dot(a, b, preferred_element_type=jnp.float32)


def lag_kernel(valid_ref, own, core, across, corner, near, fh, fl, ih, il, out, spec, power):
    tm = lax.axis_index("tm")
    z, q = tm // GROUP, tm % GROUP
    lower = q < 2
    valid = valid_ref[0]
    frame = lax.broadcasted_iota(jnp.int32, (FRAMES, LANES), 0)

    def transform(ref, slot, block):
        keep = frame + block * FRAMES < valid
        part = [
            jnp.where(keep, ref[k].astype(jnp.float32), 0.0).astype(jnp.bfloat16)
            for k in range(3)
        ]
        clean = jnp.concatenate(part, axis=1)
        spec[slot] = dot(fh[...], clean) + dot(fl[...], clean)

    base = z * GROUP
    transform(own, q, base + q)
    transform(core, q ^ 1, base + (q ^ 1))
    transform(near, GROUP, jnp.where(lower, base + GROUP, base - 1))
    transform(across, q ^ 2, base + (q ^ 2))
    transform(corner, q ^ 3, base + (q ^ 3))

    first = jnp.where(lower, 3, 4)
    second = jnp.where(lower, 4, 0)
    half = SIZE // 2
    rows = 8
    for parity in range(2):

        def step(r, carry):
            at = pl.multiple_of(parity * (half // 2) + r * rows, rows)
            re = lambda j: spec[j, pl.ds(at, rows), :]
            im = lambda j: spec[j, pl.ds(half + at, rows), :]
            a = [(re(j), im(j)) for j in range(GROUP)]
            same = sum(x * x + y * y for x, y in a)
            pairs = [(a[0], a[1]), (a[1], a[2]), (a[2], a[3])]
            pairs.append(((re(first), im(first)), (re(second), im(second))))
            cr = sum(x[0] * y[1] - x[1] * y[0] for x, y in pairs)
            ci = sum(x[0] * y[0] + x[1] * y[1] for x, y in pairs)
            pr = same + cr if parity == 0 else same - cr
            pi = -ci if parity == 0 else ci
            fold = lambda t: t[:, :LANES] + t[:, LANES : 2 * LANES] + t[:, 2 * LANES :]
            power[pl.ds(at, rows), :] = fold(pr)
            power[pl.ds(half + at, rows), :] = fold(pi)
            return carry

        lax.fori_loop(0, half // 2 // rows, step, 0)

    p = power[...]
    ph = p.astype(jnp.bfloat16)
    pl_ = (p - ph.astype(jnp.float32)).astype(jnp.bfloat16)
    out[...] = dot(ih[...], ph) + (dot(il[...], ph) + dot(ih[...], pl_))


def lag_sums_of(valid_frames, pieces):
    (fh, fl), (ih, il) = tables()
    vmem = pl.BlockSpec(memory_space=pltpu.VMEM)
    smem = pl.BlockSpec(memory_space=pltpu.SMEM)
    return pl.pallas_call(
        lag_kernel,
        out_shape=jax.ShapeDtypeStruct((LAGS, LANES), jnp.float32),
        in_specs=[smem] + [vmem] * 9,
        out_specs=vmem,
        scratch_shapes=[
            pltpu.VMEM((GROUP + 1, SIZE, 3 * LANES), jnp.float32),
            pltpu.VMEM((SIZE, LANES), jnp.float32),
        ],
        compiler_params=pltpu.CompilerParams(vmem_limit_bytes=32 * 1024 * 1024),
        name="lag_sums",
    )(valid_frames, *pieces, fh, fl, ih, il)


def finish_kernel(valid_ref, mask_ref, parts, corr, sums):
    tm = lax.axis_index("tm")
    per = corr.shape[0]
    lag = tm * per + lax.broadcasted_iota(jnp.int32, (per, LANES), 0)
    anchors = (valid_ref[0] - lag).astype(jnp.float32)
    total = jnp.zeros((per, LANES), jnp.float32)
    count = jnp.zeros((1, LANES), jnp.float32)
    for q in range(GROUP):
        lanes = slice(q * LANES, (q + 1) * LANES)
        lag_sum = parts[q]
        for z in range(1, parts.shape[0] // GROUP):
            lag_sum = lag_sum + parts[z * GROUP + q]
        weight = mask_ref[:, lanes].astype(jnp.float32)
        value = weight * lag_sum / anchors
        corr[:, lanes] = value
        total = total + value
        count = count + weight
    row = jnp.sum(total, axis=1, keepdims=True)
    real = jnp.sum(count, axis=1, keepdims=True)
    lane = lax.broadcasted_iota(jnp.int32, (per, LANES), 1)
    line = jnp.where(lane < LANES // 2, row, real)
    sums[...] = jnp.broadcast_to(line[None], sums.shape)


def body(velocities, atom_mask, valid_frames):
    count = lax.axis_size("tm")
    q = lax.axis_index("tm") % GROUP
    by_axis = velocities.transpose(1, 0, 2)

    def piece(k):
        return lax.dynamic_slice(by_axis, (0, 0, (q ^ k) * LANES), (3, FRAMES, LANES))

    def swapped(k):
        return lax.ppermute(piece(k), "tm", [(s, s ^ k) for s in range(count)])

    own, across, corner, core = piece(0), swapped(2), swapped(3), swapped(1)
    edge = jnp.where((q == 0) | (q == 3), own, core)
    hops = [(s, s - GROUP if s % GROUP < 2 else s + GROUP) for s in range(count)]
    near = lax.ppermute(edge, "tm", [(s, d) for s, d in hops if 0 <= d < count])

    lag_sums = lag_sums_of(valid_frames, (own, core, across, corner, near))
    per = LAGS // count
    parts = lax.all_to_all(
        lag_sums.reshape(count, per, LANES), "tm", 0, 0, tiled=True
    )
    atoms = atom_mask.shape[0]
    comps = lax.axis_size("comp")
    vmem = pl.BlockSpec(memory_space=pltpu.VMEM)
    correlation, sums = pl.pallas_call(
        finish_kernel,
        out_shape=(
            jax.ShapeDtypeStruct((per, atoms), jnp.float32),
            jax.ShapeDtypeStruct((comps, per, LANES), jnp.float32),
        ),
        in_specs=[pl.BlockSpec(memory_space=pltpu.SMEM), vmem, vmem],
        out_specs=(vmem, vmem),
        name="finish",
    )(valid_frames, atom_mask.reshape(1, atoms), parts)
    everyone = lax.all_to_all(sums, "comp", 0, 0, tiled=True).sum(0)
    average = everyone[:, 0] / jnp.maximum(everyone[:, LANES // 2], 1.0)
    return correlation, average


def solution(mesh):
    return jax.shard_map(
        body,
        mesh=mesh,
        in_specs=(P("tm", None, "comp"), P("comp"), P()),
        out_specs=(P("tm", "comp"), P("tm")),
        check_vma=False,
    )
```

```python
import jax
import jax.numpy as jnp
import ml_dtypes
import numpy as np
from jax import lax
from jax.experimental import pallas as pl
from jax.experimental.pallas import tpu as pltpu
from jax.sharding import PartitionSpec as P

LAGS = 256
FRAMES = 256
SIZE = 512
LANES = 128
GROUP = 4


def two_parts(table):
    high = table.astype(ml_dtypes.bfloat16)
    low = (table - high.astype(np.float64)).astype(ml_dtypes.bfloat16)
    return high, low


def tables():
    f = np.concatenate([np.arange(0, SIZE // 2, 2), np.arange(1, SIZE // 2, 2)])
    angle = 2.0 * np.pi * (f + 0.5) / SIZE
    ahead = angle[:, None] * np.arange(FRAMES)[None, :]
    forward = np.concatenate([np.cos(ahead), -np.sin(ahead)], 0)
    back = angle[None, :] * np.arange(LAGS)[:, None]
    inverse = np.concatenate([np.cos(back), -np.sin(back)], 1) * (2.0 / SIZE)
    return two_parts(forward), two_parts(inverse)


def dot(a, b):
    return jnp.dot(a, b, preferred_element_type=jnp.float32)


def params(mib):
    return pltpu.CompilerParams(vmem_limit_bytes=mib * 1024 * 1024)


def fold(t):
    return t[:, :LANES] + t[:, LANES : 2 * LANES] + t[:, 2 * LANES :]


def transform(raw, into, slot, block, valid, fh, fl):
    frame = lax.broadcasted_iota(jnp.int32, (FRAMES, LANES), 0) + block * FRAMES
    keep = frame < valid
    part = [
        jnp.where(keep, raw[k].astype(jnp.float32), 0.0).astype(jnp.bfloat16)
        for k in range(3)
    ]
    clean = jnp.concatenate(part, axis=1)
    into[slot] = dot(fh[...], clean) + dot(fl[...], clean)


def products(power, before, selves, pairs, rows=8):
    half = SIZE // 2
    for parity in range(2):

        def step(r, carry):
            at = pl.multiple_of(parity * (half // 2) + r * rows, rows)
            read = lambda f, lo: f(pl.ds(lo + at, rows))
            both = {k: (read(f, 0), read(f, half)) for k, f in selves.items()}
            same = sum(x * x + y * y for k, (x, y) in both.items() if k[0] == "s")
            met = [(both[a], both[b]) for a, b in pairs]
            cr = sum(x[0] * y[1] - x[1] * y[0] for x, y in met)
            ci = sum(x[0] * y[0] + x[1] * y[1] for x, y in met)
            pr = fold(same + cr if parity == 0 else same - cr)
            pi = fold(-ci if parity == 0 else ci)
            if before is not None:
                pr = pr + before[pl.ds(at, rows), :]
                pi = pi + before[pl.ds(half + at, rows), :]
            power[pl.ds(at, rows), :] = pr
            power[pl.ds(half + at, rows), :] = pi
            return carry

        lax.fori_loop(0, half // 2 // rows, step, 0)


def position():
    tm = lax.axis_index("tm")
    z, q = tm // GROUP, tm % GROUP
    return z * GROUP, q // 2, q % 2


def rows_of(ref, slot):
    return lambda at: ref[slot, at, :]


def lanes_of(piece):
    return pl.ds(pl.multiple_of(piece * LANES, LANES), LANES)


def pieces_kernel(velocities, own, across, corner, core, sems):
    q = lax.axis_index("tm") % GROUP
    copies = [
        pltpu.make_async_copy(velocities.at[:, :, lanes_of(q ^ k)], out, sems.at[k])
        for k, out in ((2, across), (3, corner), (1, core), (0, own))
    ]
    for copy in copies:
        copy.start()
    for copy in copies:
        copy.wait()


def edge_kernel(own, core, out):
    q = lax.axis_index("tm") % GROUP
    mine = (q == 0) | (q == 3)

    @pl.when(mine)
    def _():
        pltpu.sync_copy(own, out)

    @pl.when(jnp.logical_not(mine))
    def _():
        pltpu.sync_copy(core, out)


def early_kernel(valid_ref, own, core, fh, fl, spec, power):
    base, pair, c = position()
    valid = valid_ref[0]
    first = base + 2 * pair
    transform(core, spec, 1 - c, first + 1 - c, valid, fh, fl)
    transform(own, spec, c, first + c, valid, fh, fl)
    blocks = {"s0": rows_of(spec, 0), "s1": rows_of(spec, 1)}
    products(power, None, blocks, [("s0", "s1")])


def late_kernel(valid_ref, across, corner, near, early, before, fh, fl, ih, il, out, spec, power):
    base, pair, c = position()
    valid = valid_ref[0]
    first = base + 2 * (1 - pair)
    beside = jnp.where(pair == 0, base + GROUP, base - 1)
    transform(near, spec, 2, beside, valid, fh, fl)
    transform(across, spec, c, first + c, valid, fh, fl)
    transform(corner, spec, 1 - c, first + 1 - c, valid, fh, fl)
    blocks = {
        "s0": rows_of(spec, 0),
        "s1": rows_of(spec, 1),
        "n": rows_of(spec, 2),
        "e": rows_of(early, 1 - pair),
    }

    @pl.when(pair == 0)
    def _():
        products(power, before, blocks, [("e", "s0"), ("s0", "s1"), ("s1", "n")])

    @pl.when(pair == 1)
    def _():
        products(power, before, blocks, [("n", "s0"), ("s0", "s1"), ("s1", "e")])

    p = power[...]
    ph = p.astype(jnp.bfloat16)
    rest = (p - ph.astype(jnp.float32)).astype(jnp.bfloat16)
    out[...] = dot(ih[...], ph) + (dot(il[...], ph) + dot(ih[...], rest))


def finish_kernel(valid_ref, mask_ref, parts, corr, sums):
    tm = lax.axis_index("tm")
    per = corr.shape[0]
    lag = tm * per + lax.broadcasted_iota(jnp.int32, (per, LANES), 0)
    anchors = (valid_ref[0] - lag).astype(jnp.float32)
    total = jnp.zeros((per, LANES), jnp.float32)
    count = jnp.zeros((1, LANES), jnp.float32)
    for q in range(GROUP):
        lanes = slice(q * LANES, (q + 1) * LANES)
        lag_sum = parts[q]
        for z in range(1, parts.shape[0] // GROUP):
            lag_sum = lag_sum + parts[z * GROUP + q]
        weight = mask_ref[:, lanes].astype(jnp.float32)
        value = weight * lag_sum / anchors
        corr[:, lanes] = value
        total = total + value
        count = count + weight
    row = jnp.sum(total, axis=1, keepdims=True)
    real = jnp.sum(count, axis=1, keepdims=True)
    lane = lax.broadcasted_iota(jnp.int32, (per, LANES), 1)
    spread = jnp.where(lane == lax.broadcasted_iota(jnp.int32, (per, LANES), 0), row, 0.0)
    line = jnp.sum(spread, axis=0, keepdims=True)
    line = jnp.where(lane[:1] < LANES // 2, line, real)
    sums[...] = jnp.broadcast_to(line[None], sums.shape)


def average_kernel(sums, out):
    line = jnp.sum(sums[...], axis=0)
    lane = lax.broadcasted_iota(jnp.int32, line.shape, 1)
    real = jnp.max(jnp.where(lane == LANES - 1, line, 0.0), axis=1, keepdims=True)
    out[...] = (line / jnp.maximum(real, 1.0))[0, : out.shape[0]]


def body(velocities, atom_mask, valid_frames):
    count = lax.axis_size("tm")
    comps = lax.axis_size("comp")
    atoms = atom_mask.shape[0]
    per = LAGS // count
    by_axis = velocities.transpose(1, 0, 2)
    anywhere = pl.BlockSpec(memory_space=pl.ANY)
    vmem = pl.BlockSpec(memory_space=pltpu.VMEM)
    smem = pl.BlockSpec(memory_space=pltpu.SMEM)
    block = jax.ShapeDtypeStruct((3, FRAMES, LANES), velocities.dtype)
    f32 = lambda *shape: jax.ShapeDtypeStruct(shape, jnp.float32)
    cost = lambda n: pl.CostEstimate(flops=0, bytes_accessed=n, transcendentals=0)

    own, to_across, to_corner, to_core = pl.pallas_call(
        pieces_kernel,
        out_shape=(block,) * 4,
        in_specs=[anywhere],
        out_specs=(anywhere,) * 4,
        scratch_shapes=[pltpu.SemaphoreType.DMA((GROUP,))],
        compiler_params=params(1),
        name="pieces",
    )(by_axis)

    def swapped(k, piece):
        return lax.ppermute(piece, "tm", [(s, s ^ k) for s in range(count)])

    across, corner, core = swapped(2, to_across), swapped(3, to_corner), swapped(1, to_core)
    edge = pl.pallas_call(
        edge_kernel,
        out_shape=block,
        in_specs=[anywhere] * 2,
        out_specs=anywhere,
        compiler_params=params(1),
        cost_estimate=cost(2 * 3 * FRAMES * LANES * 2),
        name="edge",
    )(own, core)
    hops = [(s, s - GROUP if s % GROUP < 2 else s + GROUP) for s in range(count)]
    near = lax.ppermute(edge, "tm", [(s, d) for s, d in hops if 0 <= d < count])

    (fh, fl), (ih, il) = tables()
    early, before = pl.pallas_call(
        early_kernel,
        out_shape=(f32(2, SIZE, 3 * LANES), f32(SIZE, LANES)),
        in_specs=[smem] + [vmem] * 4,
        out_specs=(vmem, vmem),
        compiler_params=params(16),
        cost_estimate=cost(8_000_000),
        name="early_blocks",
    )(valid_frames, own, core, fh, fl)
    lag_sums = pl.pallas_call(
        late_kernel,
        out_shape=f32(LAGS, LANES),
        in_specs=[smem] + [vmem] * 9,
        out_specs=vmem,
        scratch_shapes=[
            pltpu.VMEM((3, SIZE, 3 * LANES), jnp.float32),
            pltpu.VMEM((SIZE, LANES), jnp.float32),
        ],
        compiler_params=params(16),
        name="lag_sums",
    )(valid_frames, across, corner, near, early, before, fh, fl, ih, il)

    parts = lax.all_to_all(
        lag_sums.reshape(count, per, LANES), "tm", 0, 0, tiled=True
    )
    correlation, sums = pl.pallas_call(
        finish_kernel,
        out_shape=(f32(per, atoms), f32(comps, 1, LANES)),
        in_specs=[smem, vmem, vmem],
        out_specs=(vmem, vmem),
        compiler_params=params(2),
        name="finish",
    )(valid_frames, atom_mask.reshape(1, atoms), parts)
    everyone = lax.all_to_all(sums, "comp", 0, 0, tiled=True)
    average = pl.pallas_call(
        average_kernel,
        out_shape=f32(per),
        in_specs=[vmem],
        out_specs=vmem,
        compiler_params=params(1),
        name="average",
    )(everyone)
    return correlation, average


def solution(mesh):
    return jax.shard_map(
        body,
        mesh=mesh,
        in_specs=(P("tm", None, "comp"), P("comp"), P()),
        out_specs=(P("tm", "comp"), P("tm")),
        check_vma=False,
    )
```

```python
import functools

import jax
import jax.numpy as jnp
import ml_dtypes
import numpy as np
from jax import lax
from jax.experimental import pallas as pl
from jax.experimental.pallas import tpu as pltpu
from jax.sharding import PartitionSpec as P

LAGS = 256
FRAMES = 256
SIZE = 512
LANES = 128
GROUP = 4


def two_parts(table):
    high = table.astype(ml_dtypes.bfloat16)
    low = (table - high.astype(np.float64)).astype(ml_dtypes.bfloat16)
    return high, low


def tables():
    f = np.concatenate([np.arange(0, SIZE // 2, 2), np.arange(1, SIZE // 2, 2)])
    angle = 2.0 * np.pi * (f + 0.5) / SIZE
    ahead = angle[:, None] * np.arange(FRAMES)[None, :]
    forward = np.concatenate([np.cos(ahead), -np.sin(ahead)], 0)
    back = angle[None, :] * np.arange(LAGS)[:, None]
    inverse = np.concatenate([np.cos(back), -np.sin(back)], 1) * (2.0 / SIZE)
    return two_parts(forward), two_parts(inverse)


def dot(a, b):
    return jnp.dot(a, b, preferred_element_type=jnp.float32)


def params(mib):
    return pltpu.CompilerParams(vmem_limit_bytes=mib * 1024 * 1024)


def fold(t):
    return t[:, :LANES] + t[:, LANES : 2 * LANES] + t[:, 2 * LANES :]


def transform(raw, into, slot, block, valid, fh, fl):
    frame = lax.broadcasted_iota(jnp.int32, (FRAMES, LANES), 0) + block * FRAMES
    keep = frame < valid
    part = [
        jnp.where(keep, raw[k].astype(jnp.float32), 0.0).astype(jnp.bfloat16)
        for k in range(3)
    ]
    clean = jnp.concatenate(part, axis=1)
    into[slot] = dot(fh[...], clean) + dot(fl[...], clean)


def products(power, before, blocks, alone, pairs, rows=8):
    half = SIZE // 2
    for parity in range(2):

        def step(r, carry):
            at = pl.multiple_of(parity * (half // 2) + r * rows, rows)
            read = lambda f, lo: f(pl.ds(lo + at, rows))
            both = [(read(f, 0), read(f, half)) for f in blocks]
            same = sum(both[k][0] * both[k][0] + both[k][1] * both[k][1] for k in alone)
            met = [(both[a], both[b]) for a, b in pairs]
            pr, pi = fold(same), 0.0
            if met:
                cr = fold(sum(x[0] * y[1] - x[1] * y[0] for x, y in met))
                ci = fold(sum(x[0] * y[0] + x[1] * y[1] for x, y in met))
                pr, pi = (pr + cr, -ci) if parity == 0 else (pr - cr, ci)
            if before is not None:
                pr = pr + before[pl.ds(at, rows), :]
                pi = pi + before[pl.ds(half + at, rows), :]
            power[pl.ds(at, rows), :] = pr
            power[pl.ds(half + at, rows), :] = pi
            return carry

        lax.fori_loop(0, half // 2 // rows, step, 0)


def position():
    tm = lax.axis_index("tm")
    z, q = tm // GROUP, tm % GROUP
    return z * GROUP, q // 2, q % 2


def rows_of(ref, slot):
    return lambda at: ref[slot, at, :]


def lanes_of(piece):
    return pl.ds(pl.multiple_of(piece * LANES, LANES), LANES)


def pieces_kernel(which, velocities, *rest):
    *outs, sems = rest
    q = lax.axis_index("tm") % GROUP
    copies = [
        pltpu.make_async_copy(velocities.at[:, :, lanes_of(q ^ k)], out, sems.at[n])
        for n, (k, out) in enumerate(zip(which, outs))
    ]
    for copy in copies:
        copy.start()
    for copy in copies:
        copy.wait()


def edge_kernel(own, core, out):
    q = lax.axis_index("tm") % GROUP
    mine = (q == 0) | (q == 3)

    @pl.when(mine)
    def _():
        pltpu.sync_copy(own, out)

    @pl.when(jnp.logical_not(mine))
    def _():
        pltpu.sync_copy(core, out)


def early_kernel(valid_ref, own, core, fh, fl, spec, power):
    base, pair, c = position()
    valid = valid_ref[0]
    first = base + 2 * pair
    transform(core, spec, 1 - c, first + 1 - c, valid, fh, fl)
    transform(own, spec, c, first + c, valid, fh, fl)
    products(power, None, [rows_of(spec, 0), rows_of(spec, 1)], [0, 1], [(0, 1)])


def in_order(case, early, near, across, corner):
    ends = [rows_of(early, 1 - case // 2), near]
    late = [across, corner]
    if case // 2:
        ends.reverse()
    if case % 2:
        late.reverse()
    return [ends[0], *late, ends[1]]


def middle_kernel(valid_ref, near, across, early, before, fh, fl, spec, power):
    base, pair, c = position()
    valid = valid_ref[0]
    beside = jnp.where(pair == 0, base + GROUP, base - 1)
    transform(near, spec, 1, beside, valid, fh, fl)
    transform(across, spec, 0, base + 2 * (1 - pair) + c, valid, fh, fl)
    for case in range(GROUP):
        line = in_order(case, early, rows_of(spec, 1), rows_of(spec, 0), None)
        line = line[2:] if case % 2 else line[:2]

        @pl.when(2 * pair + c == case)
        def _(line=line, case=case):
            products(power, before, line, [1 - case % 2], [(0, 1)])


def late_kernel(valid_ref, corner, early, middle, before, fh, fl, ih, il, out, spec, power):
    base, pair, c = position()
    block = base + 2 * (1 - pair) + 1 - c
    transform(corner, spec, 0, block, valid_ref[0], fh, fl)
    for case in range(GROUP):
        line = in_order(case, early, rows_of(middle, 1), rows_of(middle, 0), rows_of(spec, 0))
        line = line[:3] if case % 2 else line[1:]

        @pl.when(2 * pair + c == case)
        def _(line=line):
            products(power, before, line, [1], [(0, 1), (1, 2)])

    p = power[...]
    ph = p.astype(jnp.bfloat16)
    rest = (p - ph.astype(jnp.float32)).astype(jnp.bfloat16)
    both = dot(ih[...], jnp.concatenate([ph, rest], axis=1))
    out[...] = both[:, :LANES] + (dot(il[...], ph) + both[:, LANES:])


def correlations(valid_ref, mask_ref, parts):
    per = parts.shape[1]
    lag = lax.axis_index("tm") * per + lax.broadcasted_iota(jnp.int32, (per, LANES), 0)
    anchors = (valid_ref[0] - lag).astype(jnp.float32)
    for q in range(GROUP):
        lag_sum = parts[q]
        for z in range(1, parts.shape[0] // GROUP):
            lag_sum = lag_sum + parts[z * GROUP + q]
        weight = mask_ref[:, q * LANES : (q + 1) * LANES].astype(jnp.float32)
        yield q, weight, weight * lag_sum / anchors


def sums_kernel(valid_ref, mask_ref, parts, sums):
    per = parts.shape[1]
    total = jnp.zeros((per, LANES), jnp.float32)
    count = jnp.zeros((1, LANES), jnp.float32)
    for _, weight, value in correlations(valid_ref, mask_ref, parts):
        total = total + value
        count = count + weight
    row = jnp.sum(total, axis=1, keepdims=True)
    real = jnp.sum(count, axis=1, keepdims=True)
    lane = lax.broadcasted_iota(jnp.int32, (per, LANES), 1)
    spread = jnp.where(lane == lax.broadcasted_iota(jnp.int32, (per, LANES), 0), row, 0.0)
    line = jnp.sum(spread, axis=0, keepdims=True)
    line = jnp.where(lane[:1] < LANES // 2, line, real)
    sums[...] = jnp.broadcast_to(line[None], sums.shape)


def finish_kernel(valid_ref, mask_ref, parts, everyone, corr, average):
    for q, _, value in correlations(valid_ref, mask_ref, parts):
        corr[:, q * LANES : (q + 1) * LANES] = value
    line = jnp.sum(everyone[...], axis=0)
    lane = lax.broadcasted_iota(jnp.int32, line.shape, 1)
    real = jnp.max(jnp.where(lane == LANES - 1, line, 0.0), axis=1, keepdims=True)
    average[...] = (line / jnp.maximum(real, 1.0))[0, : average.shape[0]]


def body(velocities, atom_mask, valid_frames):
    count = lax.axis_size("tm")
    comps = lax.axis_size("comp")
    atoms = atom_mask.shape[0]
    per = LAGS // count
    by_axis = velocities.transpose(1, 0, 2)
    anywhere = pl.BlockSpec(memory_space=pl.ANY)
    vmem = pl.BlockSpec(memory_space=pltpu.VMEM)
    smem = pl.BlockSpec(memory_space=pltpu.SMEM)
    block = jax.ShapeDtypeStruct((3, FRAMES, LANES), velocities.dtype)
    f32 = lambda *shape: jax.ShapeDtypeStruct(shape, jnp.float32)
    cost = lambda n: pl.CostEstimate(flops=0, bytes_accessed=n, transcendentals=0)

    order = (1, 2, 3, 0)
    to_core, to_across, to_corner, own = pl.pallas_call(
        functools.partial(pieces_kernel, order),
        out_shape=(block,) * len(order),
        in_specs=[anywhere],
        out_specs=(anywhere,) * len(order),
        scratch_shapes=[pltpu.SemaphoreType.DMA((len(order),))],
        compiler_params=params(53),
        name="pieces",
    )(by_axis)

    def swapped(k, piece):
        return lax.ppermute(piece, "tm", [(s, s ^ k) for s in range(count)])

    core, across, corner = swapped(1, to_core), swapped(2, to_across), swapped(3, to_corner)
    edge = pl.pallas_call(
        edge_kernel,
        out_shape=block,
        in_specs=[anywhere] * 2,
        out_specs=anywhere,
        compiler_params=params(1),
        cost_estimate=cost(2 * 3 * FRAMES * LANES * 2),
        name="edge",
    )(own, core)
    hops = [(s, s - GROUP if s % GROUP < 2 else s + GROUP) for s in range(count)]
    near = lax.ppermute(edge, "tm", [(s, d) for s, d in hops if 0 <= d < count])

    (fh, fl), (ih, il) = tables()
    early, before = pl.pallas_call(
        early_kernel,
        out_shape=(f32(2, SIZE, 3 * LANES), f32(SIZE, LANES)),
        in_specs=[smem] + [vmem] * 4,
        out_specs=(vmem, vmem),
        compiler_params=params(16),
        cost_estimate=cost(8_000_000),
        name="early_blocks",
    )(valid_frames, own, core, fh, fl)
    middle, before = pl.pallas_call(
        middle_kernel,
        out_shape=(f32(2, SIZE, 3 * LANES), f32(SIZE, LANES)),
        in_specs=[smem] + [vmem] * 6,
        out_specs=(vmem, vmem),
        compiler_params=params(8),
        name="middle_block",
    )(valid_frames, near, across, early, before, fh, fl)
    lag_sums = pl.pallas_call(
        late_kernel,
        out_shape=f32(LAGS, LANES),
        in_specs=[smem] + [vmem] * 8,
        out_specs=vmem,
        scratch_shapes=[
            pltpu.VMEM((1, SIZE, 3 * LANES), jnp.float32),
            pltpu.VMEM((SIZE, LANES), jnp.float32),
        ],
        compiler_params=params(16),
        name="lag_sums",
    )(valid_frames, corner, early, middle, before, fh, fl, ih, il)

    parts = lax.all_to_all(
        lag_sums.reshape(count, per, LANES), "tm", 0, 0, tiled=True
    )
    mask = atom_mask.reshape(1, atoms)
    sums = pl.pallas_call(
        sums_kernel,
        out_shape=f32(comps, 1, LANES),
        in_specs=[smem, vmem, vmem],
        out_specs=vmem,
        compiler_params=params(2),
        name="sums",
    )(valid_frames, mask, parts)
    everyone = lax.all_to_all(sums, "comp", 0, 0, tiled=True)
    correlation, average = pl.pallas_call(
        finish_kernel,
        out_shape=(f32(per, atoms), f32(per)),
        in_specs=[smem, vmem, vmem, vmem],
        out_specs=(vmem, vmem),
        compiler_params=params(2),
        name="finish",
    )(valid_frames, mask, parts, everyone)
    return correlation, average


def solution(mesh):
    return jax.shard_map(
        body,
        mesh=mesh,
        in_specs=(P("tm", None, "comp"), P("comp"), P()),
        out_specs=(P("tm", "comp"), P("tm")),
        check_vma=False,
    )
```

```python
import functools

import jax
import jax.numpy as jnp
import ml_dtypes
import numpy as np
from jax import lax
from jax.experimental import pallas as pl
from jax.experimental.pallas import tpu as pltpu
from jax.sharding import PartitionSpec as P

LAGS = 256
FRAMES = 256
SIZE = 512
LANES = 128
GROUP = 4


def two_parts(table):
    high = table.astype(ml_dtypes.bfloat16)
    low = (table - high.astype(np.float64)).astype(ml_dtypes.bfloat16)
    return high, low


def tables():
    f = np.concatenate([np.arange(0, SIZE // 2, 2), np.arange(1, SIZE // 2, 2)])
    angle = 2.0 * np.pi * (f + 0.5) / SIZE
    ahead = angle[:, None] * np.arange(FRAMES)[None, :]
    forward = np.concatenate([np.cos(ahead), -np.sin(ahead)], 0)
    back = angle[None, :] * np.arange(LAGS)[:, None]
    inverse = np.concatenate([np.cos(back), -np.sin(back)], 1) * (2.0 / SIZE)
    return two_parts(forward), two_parts(inverse)


def dot(a, b):
    return jnp.dot(a, b, preferred_element_type=jnp.float32)


def params(mib):
    return pltpu.CompilerParams(vmem_limit_bytes=mib * 1024 * 1024)


def fold(t):
    return t[:, :LANES] + t[:, LANES : 2 * LANES] + t[:, 2 * LANES :]


def transform(raw, into, slot, block, valid, fh, fl):
    frame = lax.broadcasted_iota(jnp.int32, (FRAMES, LANES), 0) + block * FRAMES
    keep = frame < valid
    part = [
        jnp.where(keep, raw[k].astype(jnp.float32), 0.0).astype(jnp.bfloat16)
        for k in range(3)
    ]
    clean = jnp.concatenate(part, axis=1)
    into[slot] = dot(fh[...], clean) + dot(fl[...], clean)


def products(power, before, blocks, alone, pairs, rows=8):
    half = SIZE // 2
    for parity in range(2):

        def step(r, carry):
            at = pl.multiple_of(parity * (half // 2) + r * rows, rows)
            read = lambda f, lo: f(pl.ds(lo + at, rows))
            both = [(read(f, 0), read(f, half)) for f in blocks]
            same = sum(both[k][0] * both[k][0] + both[k][1] * both[k][1] for k in alone)
            met = [(both[a], both[b]) for a, b in pairs]
            pr, pi = fold(same), 0.0
            if met:
                cr = fold(sum(x[0] * y[1] - x[1] * y[0] for x, y in met))
                ci = fold(sum(x[0] * y[0] + x[1] * y[1] for x, y in met))
                pr, pi = (pr + cr, -ci) if parity == 0 else (pr - cr, ci)
            if before is not None:
                pr = pr + before[pl.ds(at, rows), :]
                pi = pi + before[pl.ds(half + at, rows), :]
            power[pl.ds(at, rows), :] = pr
            power[pl.ds(half + at, rows), :] = pi
            return carry

        lax.fori_loop(0, half // 2 // rows, step, 0)


def position():
    tm = lax.axis_index("tm")
    z, q = tm // GROUP, tm % GROUP
    return z * GROUP, q // 2, q % 2


def rows_of(ref, slot):
    return lambda at: ref[slot, at, :]


def lanes_of(piece):
    return pl.ds(pl.multiple_of(piece * LANES, LANES), LANES)


def pieces_kernel(which, velocities, *rest):
    *outs, sems = rest
    q = lax.axis_index("tm") % GROUP
    copies = [
        pltpu.make_async_copy(velocities.at[:, :, lanes_of(q ^ k)], out, sems.at[n])
        for n, (k, out) in enumerate(zip(which, outs))
    ]
    for copy in copies:
        copy.start()
    for copy in copies:
        copy.wait()


def edge_kernel(own, core, out):
    q = lax.axis_index("tm") % GROUP
    mine = (q == 0) | (q == 3)

    @pl.when(mine)
    def _():
        pltpu.sync_copy(own, out)

    @pl.when(jnp.logical_not(mine))
    def _():
        pltpu.sync_copy(core, out)


def early_kernel(valid_ref, own, core, fh, fl, spec, power):
    base, pair, c = position()
    valid = valid_ref[0]
    first = base + 2 * pair
    transform(core, spec, 1 - c, first + 1 - c, valid, fh, fl)
    transform(own, spec, c, first + c, valid, fh, fl)
    products(power, None, [rows_of(spec, 0), rows_of(spec, 1)], [0, 1], [(0, 1)])


def in_order(case, early, near, across, corner):
    ends = [rows_of(early, 1 - case // 2), near]
    late = [across, corner]
    if case // 2:
        ends.reverse()
    if case % 2:
        late.reverse()
    return [ends[0], *late, ends[1]]


def middle_kernel(valid_ref, near, across, early, before, fh, fl, spec, power):
    base, pair, c = position()
    valid = valid_ref[0]
    blocks = lax.axis_size("tm")
    beside = jnp.where(pair == 0, base + GROUP, jnp.where(base == 0, blocks, base - 1))
    transform(near, spec, 1, beside, valid, fh, fl)
    transform(across, spec, 0, base + 2 * (1 - pair) + c, valid, fh, fl)
    for case in range(GROUP):
        line = in_order(case, early, rows_of(spec, 1), rows_of(spec, 0), None)
        line = line[2:] if case % 2 else line[:2]

        @pl.when(2 * pair + c == case)
        def _(line=line, case=case):
            products(power, before, line, [1 - case % 2], [(0, 1)])


def late_kernel(valid_ref, corner, early, middle, before, fh, fl, ih, il, out, spec, power):
    base, pair, c = position()
    block = base + 2 * (1 - pair) + 1 - c
    transform(corner, spec, 0, block, valid_ref[0], fh, fl)
    for case in range(GROUP):
        line = in_order(case, early, rows_of(middle, 1), rows_of(middle, 0), rows_of(spec, 0))
        line = line[:3] if case % 2 else line[1:]

        @pl.when(2 * pair + c == case)
        def _(line=line):
            products(power, before, line, [1], [(0, 1), (1, 2)])

    p = power[...]
    ph = p.astype(jnp.bfloat16)
    rest = (p - ph.astype(jnp.float32)).astype(jnp.bfloat16)
    both = dot(ih[...], jnp.concatenate([ph, rest], axis=1))
    out[...] = both[:, :LANES] + (dot(il[...], ph) + both[:, LANES:])


def correlations(valid_ref, mask_ref, parts):
    per = parts.shape[1]
    lag = lax.axis_index("tm") * per + lax.broadcasted_iota(jnp.int32, (per, LANES), 0)
    anchors = (valid_ref[0] - lag).astype(jnp.float32)
    for q in range(GROUP):
        lag_sum = parts[q]
        for z in range(1, parts.shape[0] // GROUP):
            lag_sum = lag_sum + parts[z * GROUP + q]
        weight = mask_ref[:, q * LANES : (q + 1) * LANES].astype(jnp.float32)
        yield q, weight, weight * lag_sum / anchors


def sums_kernel(valid_ref, mask_ref, parts, sums):
    per = parts.shape[1]
    total = jnp.zeros((per, LANES), jnp.float32)
    count = jnp.zeros((1, LANES), jnp.float32)
    for _, weight, value in correlations(valid_ref, mask_ref, parts):
        total = total + value
        count = count + weight
    row = jnp.sum(total, axis=1, keepdims=True)
    real = jnp.sum(count, axis=1, keepdims=True)
    lane = lax.broadcasted_iota(jnp.int32, (per, LANES), 1)
    spread = jnp.where(lane == lax.broadcasted_iota(jnp.int32, (per, LANES), 0), row, 0.0)
    line = jnp.sum(spread, axis=0, keepdims=True)
    line = jnp.where(lane[:1] < LANES // 2, line, real)
    sums[...] = jnp.broadcast_to(line[None], sums.shape)


def finish_kernel(valid_ref, mask_ref, parts, everyone, corr, average):
    for q, _, value in correlations(valid_ref, mask_ref, parts):
        corr[:, q * LANES : (q + 1) * LANES] = value
    line = jnp.sum(everyone[...], axis=0)
    lane = lax.broadcasted_iota(jnp.int32, line.shape, 1)
    real = jnp.max(jnp.where(lane == LANES - 1, line, 0.0), axis=1, keepdims=True)
    average[...] = (line / jnp.maximum(real, 1.0))[0, : average.shape[0]]


def body(velocities, atom_mask, valid_frames):
    count = lax.axis_size("tm")
    comps = lax.axis_size("comp")
    atoms = atom_mask.shape[0]
    per = LAGS // count
    by_axis = velocities.transpose(1, 0, 2)
    anywhere = pl.BlockSpec(memory_space=pl.ANY)
    vmem = pl.BlockSpec(memory_space=pltpu.VMEM)
    smem = pl.BlockSpec(memory_space=pltpu.SMEM)
    block = jax.ShapeDtypeStruct((3, FRAMES, LANES), velocities.dtype)
    f32 = lambda *shape: jax.ShapeDtypeStruct(shape, jnp.float32)
    cost = lambda n: pl.CostEstimate(flops=0, bytes_accessed=n, transcendentals=0)

    order = (1, 2, 3, 0)
    to_core, to_across, to_corner, own = pl.pallas_call(
        functools.partial(pieces_kernel, order),
        out_shape=(block,) * len(order),
        in_specs=[anywhere],
        out_specs=(anywhere,) * len(order),
        scratch_shapes=[pltpu.SemaphoreType.DMA((len(order),))],
        compiler_params=params(53),
        name="pieces",
    )(by_axis)

    def swapped(k, piece):
        return lax.ppermute(piece, "tm", [(s, s ^ k) for s in range(count)])

    core, across, corner = swapped(1, to_core), swapped(2, to_across), swapped(3, to_corner)
    edge = pl.pallas_call(
        edge_kernel,
        out_shape=block,
        in_specs=[anywhere] * 2,
        out_specs=anywhere,
        compiler_params=params(1),
        cost_estimate=cost(2 * 3 * FRAMES * LANES * 2),
        name="edge",
    )(own, core)
    hops = [(s, (s - GROUP if s % GROUP < 2 else s + GROUP) % count) for s in range(count)]
    near = lax.ppermute(edge, "tm", hops)

    (fh, fl), (ih, il) = tables()
    early, before = pl.pallas_call(
        early_kernel,
        out_shape=(f32(2, SIZE, 3 * LANES), f32(SIZE, LANES)),
        in_specs=[smem] + [vmem] * 4,
        out_specs=(vmem, vmem),
        compiler_params=params(16),
        cost_estimate=cost(8_000_000),
        name="early_blocks",
    )(valid_frames, own, core, fh, fl)
    middle, before = pl.pallas_call(
        middle_kernel,
        out_shape=(f32(2, SIZE, 3 * LANES), f32(SIZE, LANES)),
        in_specs=[smem] + [vmem] * 6,
        out_specs=(vmem, vmem),
        compiler_params=params(8),
        name="middle_block",
    )(valid_frames, near, across, early, before, fh, fl)
    lag_sums = pl.pallas_call(
        late_kernel,
        out_shape=f32(LAGS, LANES),
        in_specs=[smem] + [vmem] * 8,
        out_specs=vmem,
        scratch_shapes=[
            pltpu.VMEM((1, SIZE, 3 * LANES), jnp.float32),
            pltpu.VMEM((SIZE, LANES), jnp.float32),
        ],
        compiler_params=params(16),
        name="lag_sums",
    )(valid_frames, corner, early, middle, before, fh, fl, ih, il)

    parts = lax.all_to_all(
        lag_sums.reshape(count, per, LANES), "tm", 0, 0, tiled=True
    )
    mask = atom_mask.reshape(1, atoms)
    sums = pl.pallas_call(
        sums_kernel,
        out_shape=f32(comps, 1, LANES),
        in_specs=[smem, vmem, vmem],
        out_specs=vmem,
        compiler_params=params(2),
        name="sums",
    )(valid_frames, mask, parts)
    everyone = lax.all_to_all(sums, "comp", 0, 0, tiled=True)
    correlation, average = pl.pallas_call(
        finish_kernel,
        out_shape=(f32(per, atoms), f32(per)),
        in_specs=[smem, vmem, vmem, vmem],
        out_specs=(vmem, vmem),
        compiler_params=params(2),
        name="finish",
    )(valid_frames, mask, parts, everyone)
    return correlation, average


def solution(mesh):
    return jax.shard_map(
        body,
        mesh=mesh,
        in_specs=(P("tm", None, "comp"), P("comp"), P()),
        out_specs=(P("tm", "comp"), P("tm")),
        check_vma=False,
    )
```

```python
import functools

import jax
import jax.numpy as jnp
import ml_dtypes
import numpy as np
from jax import lax
from jax.experimental import pallas as pl
from jax.experimental.pallas import tpu as pltpu
from jax.sharding import PartitionSpec as P

LAGS = 256
FRAMES = 256
SIZE = 512
LANES = 128
GROUP = 4


def two_parts(table):
    high = table.astype(ml_dtypes.bfloat16)
    low = (table - high.astype(np.float64)).astype(ml_dtypes.bfloat16)
    return high, low


def tables(order, per):
    f = np.concatenate([np.arange(0, SIZE // 2, 2), np.arange(1, SIZE // 2, 2)])
    angle = 2.0 * np.pi * (f + 0.5) / SIZE
    ahead = angle[:, None] * np.arange(FRAMES)[None, :]
    forward = np.concatenate([np.cos(ahead), -np.sin(ahead)], 0)
    lags = np.concatenate([np.arange(t * per, (t + 1) * per) for t in order])
    back = angle[None, :] * lags[:, None]
    inverse = np.concatenate([np.cos(back), -np.sin(back)], 1) * (2.0 / SIZE)
    return two_parts(forward), two_parts(inverse)


def dot(a, b):
    return jnp.dot(a, b, preferred_element_type=jnp.float32)


def params(mib):
    return pltpu.CompilerParams(vmem_limit_bytes=mib * 1024 * 1024)


def fold(t):
    return t[:, :LANES] + t[:, LANES : 2 * LANES] + t[:, 2 * LANES :]


def transform(raw, into, slot, block, valid, fh, fl):
    frame = lax.broadcasted_iota(jnp.int32, (FRAMES, LANES), 0) + block * FRAMES
    keep = frame < valid
    part = [
        jnp.where(keep, raw[k].astype(jnp.float32), 0.0).astype(jnp.bfloat16)
        for k in range(3)
    ]
    clean = jnp.concatenate(part, axis=1)
    into[slot] = dot(fh[...], clean) + dot(fl[...], clean)


def products(power, before, blocks, alone, pairs, rows=32):
    half = SIZE // 2
    for parity in range(2):

        def step(r, carry):
            at = pl.multiple_of(parity * (half // 2) + r * rows, rows)
            read = lambda f, lo: f(pl.ds(lo + at, rows))
            both = [(read(f, 0), read(f, half)) for f in blocks]
            same = sum(both[k][0] * both[k][0] + both[k][1] * both[k][1] for k in alone)
            met = [(both[a], both[b]) for a, b in pairs]
            pr, pi = fold(same), 0.0
            if met:
                cr = fold(sum(x[0] * y[1] - x[1] * y[0] for x, y in met))
                ci = fold(sum(x[0] * y[0] + x[1] * y[1] for x, y in met))
                pr, pi = (pr + cr, -ci) if parity == 0 else (pr - cr, ci)
            if before is not None:
                pr = pr + before[pl.ds(at, rows), :]
                pi = pi + before[pl.ds(half + at, rows), :]
            power[pl.ds(at, rows), :] = pr
            power[pl.ds(half + at, rows), :] = pi
            return carry

        lax.fori_loop(0, half // 2 // rows, step, 0)


def position():
    tm = lax.axis_index("tm")
    z, q = tm // GROUP, tm % GROUP
    return z * GROUP, q // 2, q % 2


def rows_of(ref, slot):
    return lambda at: ref[slot, at, :]


def lanes_of(piece):
    return pl.ds(pl.multiple_of(piece * LANES, LANES), LANES)


def pieces_kernel(which, velocities, *rest):
    *outs, sems = rest
    q = lax.axis_index("tm") % GROUP
    copies = [
        pltpu.make_async_copy(velocities.at[:, :, lanes_of(q ^ k)], out, sems.at[n])
        for n, (k, out) in enumerate(zip(which, outs))
    ]
    for copy in copies:
        copy.start()
    for copy in copies:
        copy.wait()


def edge_kernel(own, core, out):
    q = lax.axis_index("tm") % GROUP
    mine = (q == 0) | (q == 3)

    @pl.when(mine)
    def _():
        pltpu.sync_copy(own, out)

    @pl.when(jnp.logical_not(mine))
    def _():
        pltpu.sync_copy(core, out)


def early_kernel(valid_ref, own, core, fh, fl, spec, power):
    base, pair, c = position()
    valid = valid_ref[0]
    first = base + 2 * pair
    transform(core, spec, 1 - c, first + 1 - c, valid, fh, fl)
    transform(own, spec, c, first + c, valid, fh, fl)
    products(power, None, [rows_of(spec, 0), rows_of(spec, 1)], [0, 1], [(0, 1)])


def in_order(case, early, near, across, corner):
    ends = [rows_of(early, 1 - case // 2), near]
    late = [across, corner]
    if case // 2:
        ends.reverse()
    if case % 2:
        late.reverse()
    return [ends[0], *late, ends[1]]


def middle_kernel(valid_ref, near, across, early, before, fh, fl, spec, power):
    base, pair, c = position()
    valid = valid_ref[0]
    blocks = lax.axis_size("tm")
    beside = jnp.where(pair == 0, base + GROUP, jnp.where(base == 0, blocks, base - 1))
    transform(near, spec, 1, beside, valid, fh, fl)
    transform(across, spec, 0, base + 2 * (1 - pair) + c, valid, fh, fl)
    for case in range(GROUP):
        line = in_order(case, early, rows_of(spec, 1), rows_of(spec, 0), None)
        line = line[2:] if case % 2 else line[:2]

        @pl.when(2 * pair + c == case)
        def _(line=line, case=case):
            products(power, before, line, [1 - case % 2], [(0, 1)])


def late_kernel(valid_ref, corner, early, middle, before, fh, fl, ih, il, out, spec, power):
    base, pair, c = position()
    block = base + 2 * (1 - pair) + 1 - c
    transform(corner, spec, 0, block, valid_ref[0], fh, fl)
    for case in range(GROUP):
        line = in_order(case, early, rows_of(middle, 1), rows_of(middle, 0), rows_of(spec, 0))
        line = line[:3] if case % 2 else line[1:]

        @pl.when(2 * pair + c == case)
        def _(line=line):
            products(power, before, line, [1], [(0, 1), (1, 2)])

    p = power[...]
    ph = p.astype(jnp.bfloat16)
    rest = (p - ph.astype(jnp.float32)).astype(jnp.bfloat16)
    both = dot(ih[...], jnp.concatenate([ph, rest], axis=1))
    out[...] = both[:, :LANES] + (dot(il[...], ph) + both[:, LANES:])


def correlations(order, valid_ref, mask_ref, parts):
    per = parts.shape[1]
    lag = lax.axis_index("tm") * per + lax.broadcasted_iota(jnp.int32, (per, LANES), 0)
    anchors = (valid_ref[0] - lag).astype(jnp.float32)
    for q in range(GROUP):
        lag_sum = sum(parts[k] for k, source in enumerate(order) if source % GROUP == q)
        weight = mask_ref[:, q * LANES : (q + 1) * LANES].astype(jnp.float32)
        yield q, weight, weight * lag_sum / anchors


def sums_kernel(order, valid_ref, mask_ref, parts, sums):
    per = parts.shape[1]
    total = jnp.zeros((per, LANES), jnp.float32)
    count = jnp.zeros((1, LANES), jnp.float32)
    for _, weight, value in correlations(order, valid_ref, mask_ref, parts):
        total = total + value
        count = count + weight
    row = jnp.sum(total, axis=1, keepdims=True)
    real = jnp.sum(count, axis=1, keepdims=True)
    lane = lax.broadcasted_iota(jnp.int32, (per, LANES), 1)
    spread = jnp.where(lane == lax.broadcasted_iota(jnp.int32, (per, LANES), 0), row, 0.0)
    line = jnp.sum(spread, axis=0, keepdims=True)
    line = jnp.where(lane[:1] < LANES // 2, line, real)
    sums[...] = jnp.broadcast_to(line[None], sums.shape)


def finish_kernel(order, valid_ref, mask_ref, parts, everyone, corr, average):
    for q, _, value in correlations(order, valid_ref, mask_ref, parts):
        corr[:, q * LANES : (q + 1) * LANES] = value
    line = jnp.sum(everyone[...], axis=0)
    lane = lax.broadcasted_iota(jnp.int32, line.shape, 1)
    real = jnp.max(jnp.where(lane == LANES - 1, line, 0.0), axis=1, keepdims=True)
    average[...] = (line / jnp.maximum(real, 1.0))[0, : average.shape[0]]


def body(velocities, atom_mask, valid_frames):
    count = lax.axis_size("tm")
    comps = lax.axis_size("comp")
    atoms = atom_mask.shape[0]
    per = LAGS // count
    by_axis = velocities.transpose(1, 0, 2)
    anywhere = pl.BlockSpec(memory_space=pl.ANY)
    vmem = pl.BlockSpec(memory_space=pltpu.VMEM)
    smem = pl.BlockSpec(memory_space=pltpu.SMEM)
    block = jax.ShapeDtypeStruct((3, FRAMES, LANES), velocities.dtype)
    f32 = lambda *shape: jax.ShapeDtypeStruct(shape, jnp.float32)
    cost = lambda n: pl.CostEstimate(flops=0, bytes_accessed=n, transcendentals=0)

    order = (1, 2, 3, 0)
    to_core, to_across, to_corner, own = pl.pallas_call(
        functools.partial(pieces_kernel, order),
        out_shape=(block,) * len(order),
        in_specs=[anywhere],
        out_specs=(anywhere,) * len(order),
        scratch_shapes=[pltpu.SemaphoreType.DMA((len(order),))],
        compiler_params=params(53),
        name="pieces",
    )(by_axis)

    def swapped(k, piece):
        return lax.ppermute(piece, "tm", [(s, s ^ k) for s in range(count)])

    core, across, corner = swapped(1, to_core), swapped(2, to_across), swapped(3, to_corner)
    edge = pl.pallas_call(
        edge_kernel,
        out_shape=block,
        in_specs=[anywhere] * 2,
        out_specs=anywhere,
        compiler_params=params(1),
        cost_estimate=cost(2 * 3 * FRAMES * LANES * 2),
        name="edge",
    )(own, core)
    hops = [(s, (s - GROUP if s % GROUP < 2 else s + GROUP) % count) for s in range(count)]
    near = lax.ppermute(edge, "tm", hops)

    order = list(range(count))[::-1]
    (fh, fl), (ih, il) = tables(order, per)
    early, before = pl.pallas_call(
        early_kernel,
        out_shape=(f32(2, SIZE, 3 * LANES), f32(SIZE, LANES)),
        in_specs=[smem] + [vmem] * 4,
        out_specs=(vmem, vmem),
        compiler_params=params(16),
        cost_estimate=cost(8_000_000),
        name="early_blocks",
    )(valid_frames, own, core, fh, fl)
    middle, before = pl.pallas_call(
        middle_kernel,
        out_shape=(f32(2, SIZE, 3 * LANES), f32(SIZE, LANES)),
        in_specs=[smem] + [vmem] * 6,
        out_specs=(vmem, vmem),
        compiler_params=params(8),
        name="middle_block",
    )(valid_frames, near, across, early, before, fh, fl)
    lag_sums = pl.pallas_call(
        late_kernel,
        out_shape=f32(LAGS, LANES),
        in_specs=[smem] + [vmem] * 8,
        out_specs=vmem,
        scratch_shapes=[
            pltpu.VMEM((1, SIZE, 3 * LANES), jnp.float32),
            pltpu.VMEM((SIZE, LANES), jnp.float32),
        ],
        compiler_params=params(16),
        name="lag_sums",
    )(valid_frames, corner, early, middle, before, fh, fl, ih, il)

    parts = lax.all_to_all(
        lag_sums.reshape(count, per, LANES),
        "tm",
        0,
        0,
        tiled=True,
        axis_index_groups=[order],
    )
    mask = atom_mask.reshape(1, atoms)
    sums = pl.pallas_call(
        functools.partial(sums_kernel, order),
        out_shape=f32(comps, 1, LANES),
        in_specs=[smem, vmem, vmem],
        out_specs=vmem,
        compiler_params=params(2),
        name="sums",
    )(valid_frames, mask, parts)
    everyone = lax.all_to_all(
        sums, "comp", 0, 0, tiled=True, axis_index_groups=[list(range(comps))[::-1]]
    )
    correlation, average = pl.pallas_call(
        functools.partial(finish_kernel, order),
        out_shape=(f32(per, atoms), f32(per)),
        in_specs=[smem, vmem, vmem, vmem],
        out_specs=(vmem, vmem),
        compiler_params=params(2),
        name="finish",
    )(valid_frames, mask, parts, everyone)
    return correlation, average


def solution(mesh):
    return jax.shard_map(
        body,
        mesh=mesh,
        in_specs=(P("tm", None, "comp"), P("comp"), P()),
        out_specs=(P("tm", "comp"), P("tm")),
        check_vma=False,
    )
```

```python
import functools

import jax
import jax.numpy as jnp
import ml_dtypes
import numpy as np
from jax import lax
from jax.experimental import pallas as pl
from jax.experimental.pallas import tpu as pltpu
from jax.sharding import PartitionSpec as P

LAGS = 256
FRAMES = 256
SIZE = 512
LANES = 128
GROUP = 4


def two_parts(table):
    high = table.astype(ml_dtypes.bfloat16)
    low = (table - high.astype(np.float64)).astype(ml_dtypes.bfloat16)
    return high, low


def tables(order, per):
    f = np.concatenate([np.arange(0, SIZE // 2, 2), np.arange(1, SIZE // 2, 2)])
    angle = 2.0 * np.pi * (f + 0.5) / SIZE
    ahead = angle[:, None] * np.arange(FRAMES)[None, :]
    forward = np.concatenate([np.cos(ahead), -np.sin(ahead)], 0)
    lags = np.concatenate([np.arange(t * per, (t + 1) * per) for t in order])
    back = angle[None, :] * lags[:, None]
    inverse = np.concatenate([np.cos(back), -np.sin(back)], 1) * (2.0 / SIZE)
    return two_parts(forward), two_parts(inverse)


def dot(a, b):
    return jnp.dot(a, b, preferred_element_type=jnp.float32)


def params(mib):
    return pltpu.CompilerParams(vmem_limit_bytes=mib * 1024 * 1024)


def fold(t):
    return t[:, :LANES] + t[:, LANES : 2 * LANES] + t[:, 2 * LANES :]


def transform(raw, into, slot, block, valid, fh, fl):
    frame = lax.broadcasted_iota(jnp.int32, (FRAMES, LANES), 0) + block * FRAMES
    keep = frame < valid
    part = [
        jnp.where(keep, raw[k].astype(jnp.float32), 0.0).astype(jnp.bfloat16)
        for k in range(3)
    ]
    clean = jnp.concatenate(part, axis=1)
    into[slot] = dot(fh[...], clean) + dot(fl[...], clean)


def products(power, before, blocks, alone, pairs, rows=32):
    half = SIZE // 2
    for parity in range(2):

        def step(r, carry):
            at = pl.multiple_of(parity * (half // 2) + r * rows, rows)
            read = lambda f, lo: f(pl.ds(lo + at, rows))
            both = [(read(f, 0), read(f, half)) for f in blocks]
            same = sum(both[k][0] * both[k][0] + both[k][1] * both[k][1] for k in alone)
            met = [(both[a], both[b]) for a, b in pairs]
            pr, pi = fold(same), 0.0
            if met:
                cr = fold(sum(x[0] * y[1] - x[1] * y[0] for x, y in met))
                ci = fold(sum(x[0] * y[0] + x[1] * y[1] for x, y in met))
                pr, pi = (pr + cr, -ci) if parity == 0 else (pr - cr, ci)
            if before is not None:
                pr = pr + before[pl.ds(at, rows), :]
                pi = pi + before[pl.ds(half + at, rows), :]
            power[pl.ds(at, rows), :] = pr
            power[pl.ds(half + at, rows), :] = pi
            return carry

        lax.fori_loop(0, half // 2 // rows, step, 0)


def position():
    tm = lax.axis_index("tm")
    z, q = tm // GROUP, tm % GROUP
    return z * GROUP, q // 2, q % 2


def rows_of(ref, slot):
    return lambda at: ref[slot, at, :]


def lanes_of(piece):
    return pl.ds(pl.multiple_of(piece * LANES, LANES), LANES)


def pieces_kernel(which, velocities, *rest):
    *outs, sems = rest
    q = lax.axis_index("tm") % GROUP
    copies = [
        pltpu.make_async_copy(velocities.at[:, :, lanes_of(q ^ k)], out, sems.at[n])
        for n, (k, out) in enumerate(zip(which, outs))
    ]
    for copy in copies:
        copy.start()
    for copy in copies:
        copy.wait()


def edge_kernel(own, core, out):
    q = lax.axis_index("tm") % GROUP
    mine = (q == 0) | (q == 3)

    @pl.when(mine)
    def _():
        pltpu.sync_copy(own, out)

    @pl.when(jnp.logical_not(mine))
    def _():
        pltpu.sync_copy(core, out)


def early_kernel(valid_ref, own, core, fh, fl, spec, power):
    base, pair, c = position()
    valid = valid_ref[0]
    first = base + 2 * pair
    transform(core, spec, 1 - c, first + 1 - c, valid, fh, fl)
    transform(own, spec, c, first + c, valid, fh, fl)
    products(power, None, [rows_of(spec, 0), rows_of(spec, 1)], [0, 1], [(0, 1)])


def in_order(case, early, near, across, corner):
    ends = [rows_of(early, 1 - case // 2), near]
    late = [across, corner]
    if case // 2:
        ends.reverse()
    if case % 2:
        late.reverse()
    return [ends[0], *late, ends[1]]


def middle_kernel(valid_ref, near, across, early, before, fh, fl, spec, power):
    base, pair, c = position()
    valid = valid_ref[0]
    blocks = lax.axis_size("tm")
    beside = jnp.where(pair == 0, base + GROUP, jnp.where(base == 0, blocks, base - 1))
    transform(near, spec, 1, beside, valid, fh, fl)
    transform(across, spec, 0, base + 2 * (1 - pair) + c, valid, fh, fl)
    for case in range(GROUP):
        line = in_order(case, early, rows_of(spec, 1), rows_of(spec, 0), None)
        line = line[2:] if case % 2 else line[:2]

        @pl.when(2 * pair + c == case)
        def _(line=line, case=case):
            products(power, before, line, [1 - case % 2], [(0, 1)])


def late_kernel(valid_ref, corner, early, middle, before, fh, fl, ih, il, out, spec, power):
    base, pair, c = position()
    block = base + 2 * (1 - pair) + 1 - c
    transform(corner, spec, 0, block, valid_ref[0], fh, fl)
    for case in range(GROUP):
        line = in_order(case, early, rows_of(middle, 1), rows_of(middle, 0), rows_of(spec, 0))
        line = line[:3] if case % 2 else line[1:]

        @pl.when(2 * pair + c == case)
        def _(line=line):
            products(power, before, line, [1], [(0, 1), (1, 2)])

    p = power[...]
    ph = p.astype(jnp.bfloat16)
    rest = (p - ph.astype(jnp.float32)).astype(jnp.bfloat16)
    both = dot(ih[...], jnp.concatenate([ph, rest], axis=1))
    out[...] = both[:, :LANES] + (dot(il[...], ph) + both[:, LANES:])


def correlations(order, valid_ref, mask_ref, parts):
    per = parts.shape[1]
    lag = lax.axis_index("tm") * per + lax.broadcasted_iota(jnp.int32, (per, LANES), 0)
    anchors = (valid_ref[0] - lag).astype(jnp.float32)
    for q in range(GROUP):
        lag_sum = sum(parts[k] for k, source in enumerate(order) if source % GROUP == q)
        weight = mask_ref[:, q * LANES : (q + 1) * LANES].astype(jnp.float32)
        yield q, weight, weight * lag_sum / anchors


def sums_kernel(order, valid_ref, mask_ref, parts, sums):
    per = parts.shape[1]
    total = jnp.zeros((per, LANES), jnp.float32)
    count = jnp.zeros((1, LANES), jnp.float32)
    for _, weight, value in correlations(order, valid_ref, mask_ref, parts):
        total = total + value
        count = count + weight
    row = jnp.sum(total, axis=1, keepdims=True)
    real = jnp.sum(count, axis=1, keepdims=True)
    lane = lax.broadcasted_iota(jnp.int32, (per, LANES), 1)
    spread = jnp.where(lane == lax.broadcasted_iota(jnp.int32, (per, LANES), 0), row, 0.0)
    line = jnp.sum(spread, axis=0, keepdims=True)
    line = jnp.where(lane[:1] < LANES // 2, line, real)
    sums[...] = jnp.broadcast_to(line[None], sums.shape)


def finish_kernel(order, valid_ref, mask_ref, parts, everyone, corr, average):
    for q, _, value in correlations(order, valid_ref, mask_ref, parts):
        corr[:, q * LANES : (q + 1) * LANES] = value
    line = jnp.sum(everyone[...], axis=0)
    lane = lax.broadcasted_iota(jnp.int32, line.shape, 1)
    real = jnp.max(jnp.where(lane == LANES - 1, line, 0.0), axis=1, keepdims=True)
    average[...] = (line / jnp.maximum(real, 1.0))[0, : average.shape[0]]


def body(velocities, atom_mask, valid_frames):
    count = lax.axis_size("tm")
    comps = lax.axis_size("comp")
    atoms = atom_mask.shape[0]
    per = LAGS // count
    by_axis = velocities.transpose(1, 0, 2)
    anywhere = pl.BlockSpec(memory_space=pl.ANY)
    vmem = pl.BlockSpec(memory_space=pltpu.VMEM)
    smem = pl.BlockSpec(memory_space=pltpu.SMEM)
    block = jax.ShapeDtypeStruct((3, FRAMES, LANES), velocities.dtype)
    f32 = lambda *shape: jax.ShapeDtypeStruct(shape, jnp.float32)
    cost = lambda n: pl.CostEstimate(flops=0, bytes_accessed=n, transcendentals=0)

    order = (1, 2, 3, 0)
    to_core, to_across, to_corner, own = pl.pallas_call(
        functools.partial(pieces_kernel, order),
        out_shape=(block,) * len(order),
        in_specs=[anywhere],
        out_specs=(anywhere,) * len(order),
        scratch_shapes=[pltpu.SemaphoreType.DMA((len(order),))],
        compiler_params=params(53),
        name="pieces",
    )(by_axis)

    def swapped(k, piece):
        return lax.ppermute(piece, "tm", [(s, s ^ k) for s in range(count)])

    core, across, corner = swapped(1, to_core), swapped(2, to_across), swapped(3, to_corner)
    edge = pl.pallas_call(
        edge_kernel,
        out_shape=block,
        in_specs=[anywhere] * 2,
        out_specs=anywhere,
        compiler_params=params(1),
        cost_estimate=cost(2 * 3 * FRAMES * LANES * 2),
        name="edge",
    )(own, core)
    hops = [(s, (s - GROUP if s % GROUP < 2 else s + GROUP) % count) for s in range(count)]
    near = lax.ppermute(edge, "tm", hops)

    order = [z * GROUP + x * 2 + c for x in (1, 0) for z in range(count // GROUP)[::-1] for c in (1, 0)]
    (fh, fl), (ih, il) = tables(order, per)
    early, before = pl.pallas_call(
        early_kernel,
        out_shape=(f32(2, SIZE, 3 * LANES), f32(SIZE, LANES)),
        in_specs=[smem] + [vmem] * 4,
        out_specs=(vmem, vmem),
        compiler_params=params(16),
        cost_estimate=cost(8_000_000),
        name="early_blocks",
    )(valid_frames, own, core, fh, fl)
    middle, before = pl.pallas_call(
        middle_kernel,
        out_shape=(f32(2, SIZE, 3 * LANES), f32(SIZE, LANES)),
        in_specs=[smem] + [vmem] * 6,
        out_specs=(vmem, vmem),
        compiler_params=params(8),
        name="middle_block",
    )(valid_frames, near, across, early, before, fh, fl)
    lag_sums = pl.pallas_call(
        late_kernel,
        out_shape=f32(LAGS, LANES),
        in_specs=[smem] + [vmem] * 8,
        out_specs=vmem,
        scratch_shapes=[
            pltpu.VMEM((1, SIZE, 3 * LANES), jnp.float32),
            pltpu.VMEM((SIZE, LANES), jnp.float32),
        ],
        compiler_params=params(16),
        name="lag_sums",
    )(valid_frames, corner, early, middle, before, fh, fl, ih, il)

    parts = lax.all_to_all(
        lag_sums.reshape(count, per, LANES),
        "tm",
        0,
        0,
        tiled=True,
        axis_index_groups=[order],
    )
    mask = atom_mask.reshape(1, atoms)
    sums = pl.pallas_call(
        functools.partial(sums_kernel, order),
        out_shape=f32(comps, 1, LANES),
        in_specs=[smem, vmem, vmem],
        out_specs=vmem,
        compiler_params=params(2),
        name="sums",
    )(valid_frames, mask, parts)
    everyone = lax.all_to_all(
        sums, "comp", 0, 0, tiled=True, axis_index_groups=[[y * 2 + x for y in (2, 3, 1, 0) for x in (1, 0)]]
    )
    correlation, average = pl.pallas_call(
        functools.partial(finish_kernel, order),
        out_shape=(f32(per, atoms), f32(per)),
        in_specs=[smem, vmem, vmem, vmem],
        out_specs=(vmem, vmem),
        compiler_params=params(2),
        name="finish",
    )(valid_frames, mask, parts, everyone)
    return correlation, average


def solution(mesh):
    return jax.shard_map(
        body,
        mesh=mesh,
        in_specs=(P("tm", None, "comp"), P("comp"), P()),
        out_specs=(P("tm", "comp"), P("tm")),
        check_vma=False,
    )
```

```python
import functools

import jax
import jax.numpy as jnp
import ml_dtypes
import numpy as np
from jax import lax
from jax.experimental import pallas as pl
from jax.experimental.pallas import tpu as pltpu
from jax.sharding import PartitionSpec as P

LAGS = 256
FRAMES = 256
SIZE = 512
LANES = 128
GROUP = 4


def two_parts(table):
    high = table.astype(ml_dtypes.bfloat16)
    low = (table - high.astype(np.float64)).astype(ml_dtypes.bfloat16)
    return high, low


def tables(order, per):
    f = np.concatenate([np.arange(0, SIZE // 2, 2), np.arange(1, SIZE // 2, 2)])
    angle = 2.0 * np.pi * (f + 0.5) / SIZE
    ahead = angle[:, None] * np.arange(FRAMES)[None, :]
    forward = np.concatenate([np.cos(ahead), -np.sin(ahead)], 0)
    lags = np.concatenate([np.arange(t * per, (t + 1) * per) for t in order])
    back = angle[None, :] * lags[:, None]
    inverse = np.concatenate([np.cos(back), -np.sin(back)], 1) * (2.0 / SIZE)
    return two_parts(forward), two_parts(inverse)


def dot(a, b):
    return jnp.dot(a, b, preferred_element_type=jnp.float32)


def params(mib):
    return pltpu.CompilerParams(vmem_limit_bytes=mib * 1024 * 1024)


def fold(t):
    return t[:, :LANES] + t[:, LANES : 2 * LANES] + t[:, 2 * LANES :]


def transform(raw, into, slot, block, valid, fh, fl):
    frame = lax.broadcasted_iota(jnp.int32, (FRAMES, LANES), 0) + block * FRAMES
    keep = frame < valid
    part = [
        jnp.where(keep, raw[k].astype(jnp.float32), 0.0).astype(jnp.bfloat16)
        for k in range(3)
    ]
    clean = jnp.concatenate(part, axis=1)
    into[slot] = dot(fh[...], clean) + dot(fl[...], clean)


def products(power, before, blocks, alone, pairs, rows=32):
    half = SIZE // 2
    for parity in range(2):

        def step(r, carry):
            at = pl.multiple_of(parity * (half // 2) + r * rows, rows)
            read = lambda f, lo: f(pl.ds(lo + at, rows))
            both = [(read(f, 0), read(f, half)) for f in blocks]
            same = sum(both[k][0] * both[k][0] + both[k][1] * both[k][1] for k in alone)
            met = [(both[a], both[b]) for a, b in pairs]
            pr, pi = fold(same), 0.0
            if met:
                cr = fold(sum(x[0] * y[1] - x[1] * y[0] for x, y in met))
                ci = fold(sum(x[0] * y[0] + x[1] * y[1] for x, y in met))
                pr, pi = (pr + cr, -ci) if parity == 0 else (pr - cr, ci)
            if before is not None:
                pr = pr + before[pl.ds(at, rows), :]
                pi = pi + before[pl.ds(half + at, rows), :]
            power[pl.ds(at, rows), :] = pr
            power[pl.ds(half + at, rows), :] = pi
            return carry

        lax.fori_loop(0, half // 2 // rows, step, 0)


def position():
    tm = lax.axis_index("tm")
    z, q = tm // GROUP, tm % GROUP
    return z * GROUP, q // 2, q % 2


def rows_of(ref, slot):
    return lambda at: ref[slot, at, :]


def lanes_of(piece):
    return pl.ds(pl.multiple_of(piece * LANES, LANES), LANES)


def pieces_kernel(which, velocities, *rest):
    *outs, sems = rest
    q = lax.axis_index("tm") % GROUP
    copies = [
        pltpu.make_async_copy(velocities.at[:, :, lanes_of(q ^ k)], out, sems.at[n])
        for n, (k, out) in enumerate(zip(which, outs))
    ]
    for copy in copies:
        copy.start()
    for copy in copies:
        copy.wait()


def edge_kernel(own, core, out):
    q = lax.axis_index("tm") % GROUP
    mine = (q == 0) | (q == 3)

    @pl.when(mine)
    def _():
        pltpu.sync_copy(own, out)

    @pl.when(jnp.logical_not(mine))
    def _():
        pltpu.sync_copy(core, out)


def early_kernel(valid_ref, own, core, fh, fl, spec, power):
    base, pair, c = position()
    valid = valid_ref[0]
    first = base + 2 * pair
    transform(core, spec, 1 - c, first + 1 - c, valid, fh, fl)
    transform(own, spec, c, first + c, valid, fh, fl)
    products(power, None, [rows_of(spec, 0), rows_of(spec, 1)], [0, 1], [(0, 1)])


def in_order(case, early, near, across, corner):
    ends = [rows_of(early, 1 - case // 2), near]
    late = [across, corner]
    if case // 2:
        ends.reverse()
    if case % 2:
        late.reverse()
    return [ends[0], *late, ends[1]]


def middle_kernel(valid_ref, near, across, early, before, fh, fl, spec, power):
    base, pair, c = position()
    valid = valid_ref[0]
    blocks = lax.axis_size("tm")
    beside = jnp.where(pair == 0, base + GROUP, jnp.where(base == 0, blocks, base - 1))
    transform(near, spec, 1, beside, valid, fh, fl)
    transform(across, spec, 0, base + 2 * (1 - pair) + c, valid, fh, fl)
    for case in range(GROUP):
        line = in_order(case, early, rows_of(spec, 1), rows_of(spec, 0), None)
        line = line[2:] if case % 2 else line[:2]

        @pl.when(2 * pair + c == case)
        def _(line=line, case=case):
            products(power, before, line, [1 - case % 2], [(0, 1)])


def late_kernel(valid_ref, corner, early, middle, before, fh, fl, ih, il, out, spec, power):
    base, pair, c = position()
    block = base + 2 * (1 - pair) + 1 - c
    transform(corner, spec, 0, block, valid_ref[0], fh, fl)
    for case in range(GROUP):
        line = in_order(case, early, rows_of(middle, 1), rows_of(middle, 0), rows_of(spec, 0))
        line = line[:3] if case % 2 else line[1:]

        @pl.when(2 * pair + c == case)
        def _(line=line):
            products(power, before, line, [1], [(0, 1), (1, 2)])

    p = power[...]
    ph = p.astype(jnp.bfloat16)
    rest = (p - ph.astype(jnp.float32)).astype(jnp.bfloat16)
    both = dot(ih[...], jnp.concatenate([ph, rest], axis=1))
    out[...] = both[:, :LANES] + (dot(il[...], ph) + both[:, LANES:])


def correlations(order, valid_ref, mask_ref, parts):
    per = parts.shape[1]
    lag = lax.axis_index("tm") * per + lax.broadcasted_iota(jnp.int32, (per, LANES), 0)
    anchors = (valid_ref[0] - lag).astype(jnp.float32)
    for q in range(GROUP):
        lag_sum = sum(parts[k] for k, source in enumerate(order) if source % GROUP == q)
        weight = mask_ref[:, q * LANES : (q + 1) * LANES].astype(jnp.float32)
        yield q, weight, weight * lag_sum / anchors


def sums_kernel(order, valid_ref, mask_ref, parts, sums):
    per = parts.shape[1]
    total = jnp.zeros((per, LANES), jnp.float32)
    count = jnp.zeros((1, LANES), jnp.float32)
    for _, weight, value in correlations(order, valid_ref, mask_ref, parts):
        total = total + value
        count = count + weight
    row = jnp.sum(total, axis=1, keepdims=True)
    real = jnp.sum(count, axis=1, keepdims=True)
    lane = lax.broadcasted_iota(jnp.int32, (per, LANES), 1)
    spread = jnp.where(lane == lax.broadcasted_iota(jnp.int32, (per, LANES), 0), row, 0.0)
    line = jnp.sum(spread, axis=0, keepdims=True)
    line = jnp.where(lane[:1] < LANES // 2, line, real)
    sums[...] = jnp.broadcast_to(line[None], sums.shape)


def finish_kernel(order, valid_ref, mask_ref, parts, everyone, corr, average):
    for q, _, value in correlations(order, valid_ref, mask_ref, parts):
        corr[:, q * LANES : (q + 1) * LANES] = value
    line = jnp.sum(everyone[...], axis=0)
    lane = lax.broadcasted_iota(jnp.int32, line.shape, 1)
    real = jnp.max(jnp.where(lane == LANES - 1, line, 0.0), axis=1, keepdims=True)
    average[...] = (line / jnp.maximum(real, 1.0))[0, : average.shape[0]]


def body(velocities, atom_mask, valid_frames):
    count = lax.axis_size("tm")
    comps = lax.axis_size("comp")
    atoms = atom_mask.shape[0]
    per = LAGS // count
    by_axis = velocities.transpose(1, 0, 2)
    anywhere = pl.BlockSpec(memory_space=pl.ANY)
    vmem = pl.BlockSpec(memory_space=pltpu.VMEM)
    smem = pl.BlockSpec(memory_space=pltpu.SMEM)
    block = jax.ShapeDtypeStruct((3, FRAMES, LANES), velocities.dtype)
    f32 = lambda *shape: jax.ShapeDtypeStruct(shape, jnp.float32)
    cost = lambda n: pl.CostEstimate(flops=0, bytes_accessed=n, transcendentals=0)

    order = (1, 2, 3, 0)
    to_core, to_across, to_corner, own = pl.pallas_call(
        functools.partial(pieces_kernel, order),
        out_shape=(block,) * len(order),
        in_specs=[anywhere],
        out_specs=(anywhere,) * len(order),
        scratch_shapes=[pltpu.SemaphoreType.DMA((len(order),))],
        compiler_params=params(53),
        name="pieces",
    )(by_axis)

    def swapped(k, piece):
        return lax.ppermute(piece, "tm", [(s, s ^ k) for s in range(count)])

    core, across, corner = swapped(1, to_core), swapped(2, to_across), swapped(3, to_corner)
    edge = pl.pallas_call(
        edge_kernel,
        out_shape=block,
        in_specs=[anywhere] * 2,
        out_specs=anywhere,
        compiler_params=params(1),
        cost_estimate=cost(2 * 3 * FRAMES * LANES * 2),
        name="edge",
    )(own, core)
    hops = [(s, (s - GROUP if s % GROUP < 2 else s + GROUP) % count) for s in range(count)]
    near = lax.ppermute(edge, "tm", hops)

    zs = list(range(count // GROUP))[::-1]
    order = [
        z * GROUP + x * 2 + c
        for part in (zs[: len(zs) // 2], zs[len(zs) // 2 :])
        for x in (1, 0)
        for z in part
        for c in (1, 0)
    ]
    (fh, fl), (ih, il) = tables(order, per)
    early, before = pl.pallas_call(
        early_kernel,
        out_shape=(f32(2, SIZE, 3 * LANES), f32(SIZE, LANES)),
        in_specs=[smem] + [vmem] * 4,
        out_specs=(vmem, vmem),
        compiler_params=params(16),
        cost_estimate=cost(8_000_000),
        name="early_blocks",
    )(valid_frames, own, core, fh, fl)
    middle, before = pl.pallas_call(
        middle_kernel,
        out_shape=(f32(2, SIZE, 3 * LANES), f32(SIZE, LANES)),
        in_specs=[smem] + [vmem] * 6,
        out_specs=(vmem, vmem),
        compiler_params=params(8),
        name="middle_block",
    )(valid_frames, near, across, early, before, fh, fl)
    lag_sums = pl.pallas_call(
        late_kernel,
        out_shape=f32(LAGS, LANES),
        in_specs=[smem] + [vmem] * 8,
        out_specs=vmem,
        scratch_shapes=[
            pltpu.VMEM((1, SIZE, 3 * LANES), jnp.float32),
            pltpu.VMEM((SIZE, LANES), jnp.float32),
        ],
        compiler_params=params(16),
        name="lag_sums",
    )(valid_frames, corner, early, middle, before, fh, fl, ih, il)

    parts = lax.all_to_all(
        lag_sums.reshape(count, per, LANES),
        "tm",
        0,
        0,
        tiled=True,
        axis_index_groups=[order],
    )
    mask = atom_mask.reshape(1, atoms)
    sums = pl.pallas_call(
        functools.partial(sums_kernel, order),
        out_shape=f32(comps, 1, LANES),
        in_specs=[smem, vmem, vmem],
        out_specs=vmem,
        compiler_params=params(2),
        name="sums",
    )(valid_frames, mask, parts)
    everyone = lax.all_to_all(
        sums, "comp", 0, 0, tiled=True, axis_index_groups=[[y * 2 + x for y in (2, 1, 3, 0) for x in (1, 0)]]
    )
    correlation, average = pl.pallas_call(
        functools.partial(finish_kernel, order),
        out_shape=(f32(per, atoms), f32(per)),
        in_specs=[smem, vmem, vmem, vmem],
        out_specs=(vmem, vmem),
        compiler_params=params(2),
        name="finish",
    )(valid_frames, mask, parts, everyone)
    return correlation, average


def solution(mesh):
    return jax.shard_map(
        body,
        mesh=mesh,
        in_specs=(P("tm", None, "comp"), P("comp"), P()),
        out_specs=(P("tm", "comp"), P("tm")),
        check_vma=False,
    )
```

```python
import functools

import jax
import jax.numpy as jnp
import ml_dtypes
import numpy as np
from jax import lax
from jax.experimental import pallas as pl
from jax.experimental.pallas import tpu as pltpu
from jax.sharding import PartitionSpec as P

LAGS = 256
FRAMES = 256
SIZE = 512
LANES = 128
GROUP = 4


def two_parts(table):
    high = table.astype(ml_dtypes.bfloat16)
    low = (table - high.astype(np.float64)).astype(ml_dtypes.bfloat16)
    return high, low


def tables(order, per):
    f = np.concatenate([np.arange(0, SIZE // 2, 2), np.arange(1, SIZE // 2, 2)])
    angle = 2.0 * np.pi * (f + 0.5) / SIZE
    ahead = angle[:, None] * np.arange(FRAMES)[None, :]
    forward = np.concatenate([np.cos(ahead), -np.sin(ahead)], 0)
    lags = np.concatenate([np.arange(t * per, (t + 1) * per) for t in order])
    back = angle[None, :] * lags[:, None]
    inverse = np.concatenate([np.cos(back), -np.sin(back)], 1) * (2.0 / SIZE)
    return two_parts(forward), two_parts(inverse)


def dot(a, b):
    return jnp.dot(a, b, preferred_element_type=jnp.float32)


def params(mib):
    return pltpu.CompilerParams(vmem_limit_bytes=mib * 1024 * 1024)


def fold(t):
    return t[:, :LANES] + t[:, LANES : 2 * LANES] + t[:, 2 * LANES :]


def transform(raw, into, slot, block, valid, fh, fl):
    frame = lax.broadcasted_iota(jnp.int32, (FRAMES, LANES), 0) + block * FRAMES
    keep = frame < valid
    part = [
        jnp.where(keep, raw[k].astype(jnp.float32), 0.0).astype(jnp.bfloat16)
        for k in range(3)
    ]
    clean = jnp.concatenate(part, axis=1)
    into[slot] = dot(fh[...], clean) + dot(fl[...], clean)


def products(power, before, blocks, alone, pairs, rows=64):
    half = SIZE // 2
    for parity in range(2):

        def step(r, carry):
            at = pl.multiple_of(parity * (half // 2) + r * rows, rows)
            read = lambda f, lo: f(pl.ds(lo + at, rows))
            both = [(read(f, 0), read(f, half)) for f in blocks]
            same = sum(both[k][0] * both[k][0] + both[k][1] * both[k][1] for k in alone)
            met = [(both[a], both[b]) for a, b in pairs]
            pr, pi = fold(same), 0.0
            if met:
                cr = fold(sum(x[0] * y[1] - x[1] * y[0] for x, y in met))
                ci = fold(sum(x[0] * y[0] + x[1] * y[1] for x, y in met))
                pr, pi = (pr + cr, -ci) if parity == 0 else (pr - cr, ci)
            if before is not None:
                pr = pr + before[pl.ds(at, rows), :]
                pi = pi + before[pl.ds(half + at, rows), :]
            power[pl.ds(at, rows), :] = pr
            power[pl.ds(half + at, rows), :] = pi
            return carry

        lax.fori_loop(0, half // 2 // rows, step, 0)


def position():
    tm = lax.axis_index("tm")
    z, q = tm // GROUP, tm % GROUP
    return z * GROUP, q // 2, q % 2


def rows_of(ref, slot):
    return lambda at: ref[slot, at, :]


def lanes_of(piece):
    return pl.ds(pl.multiple_of(piece * LANES, LANES), LANES)


def pieces_kernel(which, velocities, *rest):
    *outs, sems = rest
    q = lax.axis_index("tm") % GROUP
    copies = [
        pltpu.make_async_copy(velocities.at[:, :, lanes_of(q ^ k)], out, sems.at[n])
        for n, (k, out) in enumerate(zip(which, outs))
    ]
    for copy in copies:
        copy.start()
    for copy in copies:
        copy.wait()


def edge_kernel(own, core, out):
    q = lax.axis_index("tm") % GROUP
    mine = (q == 0) | (q == 3)

    @pl.when(mine)
    def _():
        pltpu.sync_copy(own, out)

    @pl.when(jnp.logical_not(mine))
    def _():
        pltpu.sync_copy(core, out)


def early_kernel(valid_ref, own, core, fh, fl, spec, power):
    base, pair, c = position()
    valid = valid_ref[0]
    first = base + 2 * pair
    transform(core, spec, 1 - c, first + 1 - c, valid, fh, fl)
    transform(own, spec, c, first + c, valid, fh, fl)
    products(power, None, [rows_of(spec, 0), rows_of(spec, 1)], [0, 1], [(0, 1)])


def in_order(case, early, near, across, corner):
    ends = [rows_of(early, 1 - case // 2), near]
    late = [across, corner]
    if case // 2:
        ends.reverse()
    if case % 2:
        late.reverse()
    return [ends[0], *late, ends[1]]


def middle_kernel(valid_ref, near, across, early, before, fh, fl, spec, power):
    base, pair, c = position()
    valid = valid_ref[0]
    blocks = lax.axis_size("tm")
    beside = jnp.where(pair == 0, base + GROUP, jnp.where(base == 0, blocks, base - 1))
    transform(near, spec, 1, beside, valid, fh, fl)
    transform(across, spec, 0, base + 2 * (1 - pair) + c, valid, fh, fl)
    for case in range(GROUP):
        line = in_order(case, early, rows_of(spec, 1), rows_of(spec, 0), None)
        line = line[2:] if case % 2 else line[:2]

        @pl.when(2 * pair + c == case)
        def _(line=line, case=case):
            products(power, before, line, [1 - case % 2], [(0, 1)])


def late_kernel(valid_ref, corner, early, middle, before, fh, fl, ih, il, out, spec, power):
    base, pair, c = position()
    block = base + 2 * (1 - pair) + 1 - c
    transform(corner, spec, 0, block, valid_ref[0], fh, fl)
    for case in range(GROUP):
        line = in_order(case, early, rows_of(middle, 1), rows_of(middle, 0), rows_of(spec, 0))
        line = line[:3] if case % 2 else line[1:]

        @pl.when(2 * pair + c == case)
        def _(line=line):
            products(power, before, line, [1], [(0, 1), (1, 2)])

    p = power[...]
    ph = p.astype(jnp.bfloat16)
    rest = (p - ph.astype(jnp.float32)).astype(jnp.bfloat16)
    both = dot(ih[...], jnp.concatenate([ph, rest], axis=1))
    out[...] = both[:, :LANES] + (dot(il[...], ph) + both[:, LANES:])


def correlations(order, valid_ref, mask_ref, parts):
    per = parts.shape[1]
    lag = lax.axis_index("tm") * per + lax.broadcasted_iota(jnp.int32, (per, LANES), 0)
    anchors = (valid_ref[0] - lag).astype(jnp.float32)
    for q in range(GROUP):
        lag_sum = sum(parts[k] for k, source in enumerate(order) if source % GROUP == q)
        weight = mask_ref[:, q * LANES : (q + 1) * LANES].astype(jnp.float32)
        yield q, weight, weight * lag_sum / anchors


def sums_kernel(order, valid_ref, mask_ref, parts, sums):
    per = parts.shape[1]
    total = jnp.zeros((per, LANES), jnp.float32)
    count = jnp.zeros((1, LANES), jnp.float32)
    for _, weight, value in correlations(order, valid_ref, mask_ref, parts):
        total = total + value
        count = count + weight
    row = jnp.sum(total, axis=1, keepdims=True)
    real = jnp.sum(count, axis=1, keepdims=True)
    lane = lax.broadcasted_iota(jnp.int32, (per, LANES), 1)
    spread = jnp.where(lane == lax.broadcasted_iota(jnp.int32, (per, LANES), 0), row, 0.0)
    line = jnp.sum(spread, axis=0, keepdims=True)
    line = jnp.where(lane[:1] < LANES // 2, line, real)
    sums[...] = jnp.broadcast_to(line[None], sums.shape)


def finish_kernel(order, valid_ref, mask_ref, parts, everyone, corr, average):
    for q, _, value in correlations(order, valid_ref, mask_ref, parts):
        corr[:, q * LANES : (q + 1) * LANES] = value
    line = jnp.sum(everyone[...], axis=0)
    lane = lax.broadcasted_iota(jnp.int32, line.shape, 1)
    real = jnp.max(jnp.where(lane == LANES - 1, line, 0.0), axis=1, keepdims=True)
    average[...] = (line / jnp.maximum(real, 1.0))[0, : average.shape[0]]


def body(velocities, atom_mask, valid_frames):
    count = lax.axis_size("tm")
    comps = lax.axis_size("comp")
    atoms = atom_mask.shape[0]
    per = LAGS // count
    by_axis = velocities.transpose(1, 0, 2)
    anywhere = pl.BlockSpec(memory_space=pl.ANY)
    vmem = pl.BlockSpec(memory_space=pltpu.VMEM)
    smem = pl.BlockSpec(memory_space=pltpu.SMEM)
    block = jax.ShapeDtypeStruct((3, FRAMES, LANES), velocities.dtype)
    f32 = lambda *shape: jax.ShapeDtypeStruct(shape, jnp.float32)
    cost = lambda n: pl.CostEstimate(flops=0, bytes_accessed=n, transcendentals=0)

    order = (1, 2, 3, 0)
    to_core, to_across, to_corner, own = pl.pallas_call(
        functools.partial(pieces_kernel, order),
        out_shape=(block,) * len(order),
        in_specs=[anywhere],
        out_specs=(anywhere,) * len(order),
        scratch_shapes=[pltpu.SemaphoreType.DMA((len(order),))],
        compiler_params=params(53),
        name="pieces",
    )(by_axis)

    def swapped(k, piece):
        return lax.ppermute(piece, "tm", [(s, s ^ k) for s in range(count)])

    core, across, corner = swapped(1, to_core), swapped(2, to_across), swapped(3, to_corner)
    edge = pl.pallas_call(
        edge_kernel,
        out_shape=block,
        in_specs=[anywhere] * 2,
        out_specs=anywhere,
        compiler_params=params(1),
        cost_estimate=cost(2 * 3 * FRAMES * LANES * 2),
        name="edge",
    )(own, core)
    hops = [(s, (s - GROUP if s % GROUP < 2 else s + GROUP) % count) for s in range(count)]
    near = lax.ppermute(edge, "tm", hops)

    zs = list(range(count // GROUP))[::-1]
    order = [
        z * GROUP + x * 2 + c
        for part in (zs[: len(zs) // 2], zs[len(zs) // 2 :])
        for x in (1, 0)
        for z in part
        for c in (1, 0)
    ]
    (fh, fl), (ih, il) = tables(order, per)
    early, before = pl.pallas_call(
        early_kernel,
        out_shape=(f32(2, SIZE, 3 * LANES), f32(SIZE, LANES)),
        in_specs=[smem] + [vmem] * 4,
        out_specs=(vmem, vmem),
        compiler_params=params(16),
        cost_estimate=cost(8_000_000),
        name="early_blocks",
    )(valid_frames, own, core, fh, fl)
    middle, before = pl.pallas_call(
        middle_kernel,
        out_shape=(f32(2, SIZE, 3 * LANES), f32(SIZE, LANES)),
        in_specs=[smem] + [vmem] * 6,
        out_specs=(vmem, vmem),
        compiler_params=params(8),
        name="middle_block",
    )(valid_frames, near, across, early, before, fh, fl)
    lag_sums = pl.pallas_call(
        late_kernel,
        out_shape=f32(LAGS, LANES),
        in_specs=[smem] + [vmem] * 8,
        out_specs=vmem,
        scratch_shapes=[
            pltpu.VMEM((1, SIZE, 3 * LANES), jnp.float32),
            pltpu.VMEM((SIZE, LANES), jnp.float32),
        ],
        compiler_params=params(16),
        name="lag_sums",
    )(valid_frames, corner, early, middle, before, fh, fl, ih, il)

    parts = lax.all_to_all(
        lag_sums.reshape(count, per, LANES),
        "tm",
        0,
        0,
        tiled=True,
        axis_index_groups=[order],
    )
    mask = atom_mask.reshape(1, atoms)
    sums = pl.pallas_call(
        functools.partial(sums_kernel, order),
        out_shape=f32(comps, 1, LANES),
        in_specs=[smem, vmem, vmem],
        out_specs=vmem,
        compiler_params=params(2),
        name="sums",
    )(valid_frames, mask, parts)
    everyone = lax.all_to_all(
        sums, "comp", 0, 0, tiled=True, axis_index_groups=[[y * 2 + x for x in (1, 0) for y in (2, 1, 3, 0)]]
    )
    correlation, average = pl.pallas_call(
        functools.partial(finish_kernel, order),
        out_shape=(f32(per, atoms), f32(per)),
        in_specs=[smem, vmem, vmem, vmem],
        out_specs=(vmem, vmem),
        compiler_params=params(2),
        name="finish",
    )(valid_frames, mask, parts, everyone)
    return correlation, average


def solution(mesh):
    return jax.shard_map(
        body,
        mesh=mesh,
        in_specs=(P("tm", None, "comp"), P("comp"), P()),
        out_specs=(P("tm", "comp"), P("tm")),
        check_vma=False,
    )
```
